128 devices in a mesh: heads: 4 (over x), docs: 32 (over z, y, core).
Axes of the slice: x: 4, y: 4, z: 4, core: 2. Of those that a mesh axis runs over, the one named last changes fastest.
Arguments:
- query_rows: bfloat16 [16384, 4096], P('docs', 'heads'), may hold values from -40 to 40
- key_rows: bfloat16 [16384, 512], P('docs', 'heads'), may hold values from -4.5 to 4.5
- value_rows: bfloat16 [16384, 512], P('docs', 'heads'), may hold values from -6 to 6
- doc_blocks: int32 [16], replicated, may hold values from 1 to 16, 128 in all
- out_weight: bfloat16 [4096, 2048], P('heads', 'docs'), may hold values from -0.1875 to 0.1875
Outputs:
- mixed: bfloat16 [16384, 2048], P('docs', 'heads')
The draws below stay inside these ranges and needn't reach their ends.
All inputs are finite; a program needn't handle non-finite values.
Results may differ from the reference program's by a relative error of at most 0.0095.
Values may be sent and summed in bfloat16 or wider, within the bound.
A program may use at most 64 MiB of HBM per device.

```python
import math
import jax
import jax.numpy as jnp
import numpy as np
from jax import lax

D_MODEL = 2048
QH = 32
KVH = 4
HD = 128
BLOCK = 128
MOSTB = 16
TOK_DEV = 512
TOKENS = 16384
NBLK = 128
NDOC = 16
N_HEADS = 4


def shared_rows(key):
    base = jax.random.fold_in(key, 7)
    first_key, second_key = jax.random.split(base, 2)
    key_draw = jnp.clip(jax.random.normal(first_key, (TOKENS, KVH * HD), jnp.float32), -4.0, 4.0)
    query_draw = jnp.clip(jax.random.normal(second_key, (TOKENS, QH * HD), jnp.float32), -4.0, 4.0)
    return (query_draw, key_draw)


def draw_query_rows(key, part):
    return shared_rows(key)[0].astype(jnp.bfloat16)


def draw_key_rows(key, part):
    return shared_rows(key)[1].astype(jnp.bfloat16)


def with_spikes(array, rng, source, target, shards_of, factor):
    owner, partner = [(jnp.arange(array.shape[axis_at]) // (array.shape[axis_at] // shards_of)).reshape([-1 if axis == axis_at else 1 for axis in range(array.ndim)]) for axis_at in (source, target)]
    chosen = jax.random.permutation(rng, shards_of)[partner]
    strong = (owner == chosen) | (owner == (partner + shards_of // 2) % shards_of)
    return jnp.where(strong, factor * array, array)


def block_scale(own_key, shape, pieces, low, top_value):
    loudness = 1.0
    for axis_at, blocks in pieces:
        steps = jax.random.uniform(jax.random.fold_in(jax.random.fold_in(own_key, 6), axis_at), (blocks,), jnp.float32, low / len(pieces), top_value / len(pieces))
        loudness = loudness * jnp.repeat(jnp.exp(steps), shape[axis_at] // blocks).reshape((-1,) + (1,) * (len(shape) - 1 - axis_at))
    return loudness


def split_up(number_of, total, limit, skew):
    loads = [(1 << 20) // math.isqrt(standing ** skew) + 1 for standing in range(2, number_of + 1)]
    spare, holding = total - limit - (number_of - 1), [1] * (number_of - 1)
    while spare > 0:
        candidates = [i for i in range(number_of - 1) if holding[i] < limit]
        whole, left = sum([loads[i] for i in candidates]), spare
        for i in candidates:
            addition = min(limit - holding[i], max(1, left * loads[i] // whole), spare)
            holding[i] = holding[i] + addition
            spare = spare - addition
    return np.array([limit] + holding)


def ragged_sizes(rng, count, total, limit, skew):
    if count == 2:
        one = jax.random.randint(rng, (), max(1, total - limit), min(limit, total - 1) + 1)
        return jnp.stack([one, total - one])
    lengths = jnp.asarray(split_up(count, total, limit, skew), jnp.int32)
    couples = (count - 1) // 2
    giver, receiver = lengths[1:1 + 2 * couples:2], lengths[2:2 + 2 * couples:2]
    room = jnp.minimum(giver - 1, limit - receiver)
    moved = jax.random.randint(jax.random.fold_in(rng, 1), (couples,), 0, 1 << 20) % (room + 1)
    lengths = lengths.at[1:1 + 2 * couples:2].set(giver - moved).at[2:2 + 2 * couples:2].set(receiver + moved)
    return lengths[jax.random.permutation(jax.random.fold_in(rng, 2), count)]


def noise(key, dims, scale, reach, cuts=(), kind=jnp.bfloat16):
    values = jax.random.normal(key, dims, jnp.float32) * scale
    if len(cuts) > 0:
        values = block_scale(key, dims, cuts, -0.22, 0.18) * values
    return jnp.clip(values, min=-reach, max=reach).astype(kind)


def noise_with(own_key, extent, spread, reach, cuts, heavy, kind=jnp.bfloat16):
    array = spread * jax.random.normal(own_key, extent, jnp.float32)
    if cuts:
        array = array * block_scale(own_key, extent, cuts, -0.22, 0.18)
    return jnp.clip(with_spikes(array, jax.random.fold_in(own_key, 3), *heavy), -reach, reach).astype(kind)


def setup_inputs(seed: int = 0) -> dict:
    arg_keys = jax.random.split(jax.random.key(seed), 6)
    return {
        "query_rows": draw_query_rows(jax.random.fold_in(arg_keys[5], 71), 0),
        "key_rows": draw_key_rows(jax.random.fold_in(arg_keys[5], 71), 0),
        "value_rows": noise(arg_keys[2], (TOKENS, KVH * HD), 1.0, 6.0, ((0, 32), (1, 4))),
        "doc_blocks": ragged_sizes(arg_keys[3], NDOC, NBLK, MOSTB, 2).astype(jnp.int32),
        "out_weight": noise_with(arg_keys[4], (QH * HD, D_MODEL), (QH * HD) ** -0.5, 0.1875, ((0, 4), (1, 32)), (0, 1, 32, 2.75)),
    }


def reference(query_rows, key_rows, value_rows, doc_blocks, out_weight):
    token_count = query_rows.shape[0]
    rim_rows = (MOSTB - 1) * BLOCK
    query_block = min(512, TOK_DEV)
    window = rim_rows + query_block
    group_size = QH // KVH
    score_scale = HD ** -0.5
    doc_ends = jnp.cumsum(doc_blocks).astype(jnp.int32) * BLOCK
    positions = jnp.arange(token_count + rim_rows, dtype=jnp.int32) - rim_rows
    doc_ids = jnp.sum((doc_ends[None, :] <= positions[:, None]).astype(jnp.int32), axis=1)
    doc_ids = jnp.where(positions < 0, -1, doc_ids).astype(jnp.int32)
    padding = jnp.zeros((rim_rows, KVH * HD), key_rows.dtype)
    ext_keys = jnp.concatenate([padding, key_rows], axis=0)
    ext_values = jnp.concatenate([padding, value_rows], axis=0)

    def one_block(block_index):
        first_row = (block_index * query_block).astype(jnp.int32)
        query_part = lax.dynamic_slice_in_dim(query_rows, first_row, query_block, 0).astype(jnp.float32).reshape(query_block, KVH, group_size, HD)
        key_window = lax.dynamic_slice_in_dim(ext_keys, first_row, window, 0).astype(jnp.float32).reshape(window, KVH, HD)
        value_window = lax.dynamic_slice_in_dim(ext_values, first_row, window, 0).astype(jnp.float32).reshape(window, KVH, HD)
        query_doc = lax.dynamic_slice_in_dim(doc_ids, first_row + rim_rows, query_block, 0)
        key_doc = lax.dynamic_slice_in_dim(doc_ids, first_row, window, 0)
        query_pos = first_row + rim_rows + jnp.arange(query_block, dtype=jnp.int32)
        key_pos = first_row + jnp.arange(window, dtype=jnp.int32)
        allowed = (query_doc[:, None] == key_doc[None, :]) & (key_pos[None, :] <= query_pos[:, None])
        scores = jnp.einsum("qcgd,kcd->cgqk", query_part, key_window) * score_scale
        scores = jnp.where(allowed[None, None], scores, -jnp.inf)
        row_max = jnp.max(scores, axis=-1, keepdims=True)
        raised = jnp.exp(scores - row_max)
        row_sum = jnp.sum(raised, axis=-1)
        probs = lax.optimization_barrier(raised.astype(jnp.bfloat16)).astype(jnp.float32)
        mixed = jnp.einsum("cgqk,kcd->qcgd", probs, value_window)
        mixed = mixed / jnp.transpose(row_sum, (2, 0, 1))[..., None]
        return mixed.astype(jnp.bfloat16).reshape(query_block, QH * HD)

    blocks = lax.map(one_block, jnp.arange(token_count // query_block, dtype=jnp.int32))
    attended = blocks.reshape(token_count, QH * HD)
    feature_width = QH * HD // N_HEADS
    mixed = jnp.zeros((token_count, D_MODEL), jnp.float32)
    for head_group in range(N_HEADS):
        partial_value = jnp.dot(attended[:, head_group * feature_width:(head_group + 1) * feature_width], out_weight[head_group * feature_width:(head_group + 1) * feature_width], preferred_element_type=jnp.float32)
        mixed = mixed + lax.optimization_barrier(partial_value.astype(jnp.bfloat16)).astype(jnp.float32)
    return mixed.astype(jnp.bfloat16)
```

```python
import functools
import math

import jax
import jax.numpy as jnp
from jax import lax
from jax.experimental import pallas as pl
from jax.experimental.pallas import tpu as pltpu
from jax.sharding import PartitionSpec as P

MESH = pl.DeviceIdType.MESH
NT = (((1,), (1,)), ((), ()))
NN = (((1,), (0,)), ((), ()))
F32, BF16 = jnp.float32, jnp.bfloat16
BIG = float(2**20)
SCALE = 128**-0.5 * math.log2(math.e)
CK = 512
NC = 2048 // CK
NDOC = 16


def kernel(
    q_hbm, k_hbm, v_hbm, doc_ref, w_hbm, out_ref,
    qv, kb, eb, vv, vb, bias, wb, s_buf, att,
    ps2, pp, pm, po, r1p, r1m, r2p, r2m,
    lsem, kvs, kvr, wys, wyr, wzs, wzr, wss, wsr, xs, xr,
):
    h, d = lax.axis_index("heads"), lax.axis_index("docs")
    c, y, z = d % 2, (d // 2) % 4, d // 8
    chip = d // 2

    def at(zz, yy):
        return (h, (zz * 4 + yy) * 2 + c)

    sib = (h, d + 1 - 2 * c)
    nxt = (h, ((chip + 1) % 16) * 2 + c)
    prv = (h, ((chip + 15) % 16) * 2 + c)
    yp, ym = at(z, (y + 1) % 4), at(z, (y + 3) % 4)
    zp, zm = at((z + 1) % 4, y), at((z + 3) % 4, y)
    xp, xm = ((h + 1) % 4, d), ((h + 3) % 4, d)

    lq = pltpu.make_async_copy(q_hbm, qv, lsem.at[0])
    lk = pltpu.make_async_copy(k_hbm, kb.at[pl.ds(2048, 512), :], lsem.at[1])
    lv = pltpu.make_async_copy(v_hbm, vv, lsem.at[2])
    lw = pltpu.make_async_copy(w_hbm, wb.at[z, y, c], lsem.at[3])
    lv.start()
    lk.start()
    lw.start()
    lq.start()

    barrier = pltpu.get_barrier_semaphore()
    for other in (sib, nxt, prv, yp, ym, zp, zm, xp, xm):
        pl.semaphore_signal(barrier, inc=1, device_id=other, device_id_type=MESH)

    def remote(src, dst, ss, rs, dev):
        return pltpu.make_async_remote_copy(
            src_ref=src, dst_ref=dst, send_sem=ss, recv_sem=rs, device_id=dev, device_id_type=MESH
        )

    def kv(kind, part):
        src = (4, 2, 4 - 2 * c, 2 - 2 * c)[kind]
        dst = (2, 0, 3, 1)[kind]
        dev = (nxt, nxt, sib, sib)[kind]
        if part == 0:
            a = kb.at[pl.ds(pl.multiple_of(src * 512, 512), 512), :]
            b = kb.at[pl.ds(dst * 512, 512), :]
        else:
            a = vb.at[:, pl.ds(pl.multiple_of(src * 512, 512), 512)]
            b = vb.at[:, pl.ds(dst * 512, 512)]
        return remote(a, b, kvs.at[kind, part], kvr.at[kind, part], dev)

    def w_y(s):
        ref = wb.at[z, (y + s) % 4, c]
        return remote(ref, ref, wys.at[s], wyr.at[s], ym)

    def w_y_in(s):
        ref = wb.at[z, (y + s + 1) % 4, c]
        return remote(ref, ref, wys.at[s], wyr.at[s], ym)

    def w_z(s, k):
        row = (z, z, (z + 3) % 4, (z + 1) % 4)[k]
        ref = wb.at[row, (y + s) % 4, c]
        if k >= 2:
            ref = ref.at[pl.ds(32 * (k - 2), 32), :]
        return remote(ref, ref, wzs.at[s, k], wzr.at[s, k], (zp, zm, zp, zm)[k])

    def w_z_in(s, k):
        row = ((z + 3) % 4, (z + 1) % 4, (z + 2) % 4, (z + 2) % 4)[k]
        ref = wb.at[row, (y + s) % 4, c]
        if k >= 2:
            ref = ref.at[pl.ds(32 * (k - 2), 32), :]
        return remote(ref, ref, wzs.at[s, k], wzr.at[s, k], (zp, zm, zp, zm)[k])

    def w_s(k):
        ref = wb.at[(z + (0, 3, 1, 2)[k]) % 4, :, c]
        return remote(ref, ref, wss.at[k], wsr.at[k], sib)

    def w_s_in(k):
        ref = wb.at[(z + (0, 3, 1, 2)[k]) % 4, :, 1 - c]
        return remote(ref, ref, wss.at[k], wsr.at[k], sib)

    def w_step(s):
        if s > 0:
            w_y_in(s - 1).wait_recv()
        if s < 3:
            w_y(s).start()
        w_z(s, 0).start()
        w_z(s, 1).start()

    def w_forward(s):
        w_z_in(s, 0).wait_recv()
        w_z(s, 2).start()
        w_z_in(s, 1).wait_recv()
        w_z(s, 3).start()

    lv.wait()
    vb[:, 2048:] = jnp.transpose(vv[...].astype(F32)).astype(BF16)
    lk.wait()
    lw.wait()
    pl.semaphore_wait(barrier, 9)

    kv(0, 0).start()
    kv(0, 1).start()

    @pl.when(c == 0)
    def _():
        kv(2, 0).start()
        kv(2, 1).start()

    w_step(0)

    lane = lax.broadcasted_iota(jnp.int32, (128, 128), 1)
    row = lax.broadcasted_iota(jnp.int32, (128, 128), 0)
    for w in range(20):
        eb[w * 128 : (w + 1) * 128, :] = (lane == w).astype(F32).astype(BF16)
    tri = jnp.where(row <= lane, 0.0, -BIG).astype(F32)
    tri2 = jnp.concatenate([tri, tri], axis=1)
    first_block = d * 4
    block = lax.broadcasted_iota(jnp.int32, (16, 128), 1) + (first_block - 16)
    doc = jnp.zeros((16, 128), jnp.int32)
    own = [jnp.int32(0)] * 4
    end = jnp.int32(0)
    for t in range(NDOC):
        end = end + doc_ref[t]
        doc = doc + (end <= block).astype(jnp.int32)
        own = [own[i] + (end <= first_block + i).astype(jnp.int32) for i in range(4)]
    for i in range(4):
        allowed = (doc == own[i]) & (block >= 0)
        bias[i] = jnp.where(allowed, 0.0, -BIG).astype(BF16)

    for part in range(2):
        kv(0, part).wait_recv()
        kv(1, part).start()

        @pl.when(c == 0)
        def _():
            kv(3, part).start()

        @pl.when(c == 1)
        def _():
            kv(2, part).start()

        w_step(part + 1)
    w_forward(0)
    w_step(3)
    w_s(0).start()
    w_forward(1)
    for part in range(2):
        kv(1, part).wait_recv()

        @pl.when(c == 1)
        def _():
            kv(3, part).start()

    w_forward(2)
    lq.wait()
    for part in range(2):
        kv(2, part).wait_recv()
        kv(3, part).wait_recv()

    ones = jnp.ones((16, CK), BF16)

    def scores(i, hp, slot, ck, mx):
        k0 = pl.multiple_of((i + 1) * 128 + ck * CK, 128)
        q2 = qv[pl.ds(pl.multiple_of(i * 128, 128), 128), hp * 256 : hp * 256 + 256]
        b = jnp.concatenate([bias[i]] * 8, axis=0)
        qq = jnp.concatenate(
            [
                jnp.concatenate([q2[:, :128], b], axis=1),
                jnp.concatenate([q2[:, 128:], b], axis=1),
            ],
            axis=0,
        )
        kk = jnp.concatenate([kb[pl.ds(k0, CK), :], eb[pl.ds(k0, CK), :]], axis=1)
        s = lax.dot_general(kk, qq, NT, preferred_element_type=F32)
        if ck == NC - 1:
            s = jnp.concatenate([s[: CK - 128], s[CK - 128 :] + tri2], axis=0)
        s_buf[slot, ck * CK : (ck + 1) * CK, :] = s
        n = jnp.max(s.reshape(CK // 8, 8, 256), axis=0)
        return n if mx is None else jnp.maximum(mx, n)

    def weigh(i, slot, ck, m, acc):
        k0 = pl.multiple_of((i + 1) * 128 + ck * CK, 128)
        s = s_buf[slot, ck * CK : (ck + 1) * CK, :]
        p = jnp.exp2((s - m) * SCALE).astype(BF16)
        lhs = jnp.concatenate([vb[:, pl.ds(k0, CK)], ones], axis=0)
        t = lax.dot_general(lhs, p, NN, preferred_element_type=F32)
        return t if acc is None else acc + t

    def top(mx):
        return jnp.max(mx, axis=0, keepdims=True)

    def project(j):
        w = wb[j].reshape(512, 1024)
        return lax.dot_general(w, att[...], NN, preferred_element_type=F32)

    lo, hi = pl.ds(0, 256), pl.ds(256, 256)

    def x_copy(i, k):
        src, dst = (
            (ps2.at[i, lo], r1p.at[i]),
            (ps2.at[i, hi], r1m.at[i]),
            (pp.at[i, hi], r2p.at[i, hi]),
            (pm.at[i, lo], r2m.at[i, lo]),
            (pp.at[i, lo], r2p.at[i, lo]),
            (pm.at[i, hi], r2m.at[i, hi]),
        )[k]
        return remote(src, dst, xs.at[i, k], xr.at[i, k], (xp, xm)[k % 2])

    def merge(i):
        x_copy(i, 0).wait_recv()
        pp[i, lo, :] = (pp[i, lo, :].astype(F32) + r1p[i].astype(F32)).astype(BF16)
        x_copy(i, 4).start()
        x_copy(i, 1).wait_recv()
        pm[i, hi, :] = (pm[i, hi, :].astype(F32) + r1m[i].astype(F32)).astype(BF16)
        x_copy(i, 5).start()

    mx = None
    for ck in range(NC):
        mx = scores(0, 0, 0, ck, mx)

    def one(i, m):
        for u in range(4):
            slot = u % 2
            ni, nu = (i, u + 1) if u < 3 else (jnp.minimum(i + 1, 3), 0)
            mx, acc = None, None
            for ck in range(NC):
                mx = scores(ni, nu, 1 - slot, ck, mx)
                acc = weigh(i, slot, ck, m, acc)
            m = top(mx)
            o = (acc[:128] / acc[128:129]).astype(BF16)
            att[u * 256 : u * 256 + 128, :] = o[:, :128]
            att[u * 256 + 128 : u * 256 + 256, :] = o[:, 128:]

        @pl.when(i == 0)
        def _():
            w_forward(3)
            w_s(1).start()
            w_s(2).start()
            for s in range(4):
                w_z_in(s, 2).wait_recv()
                w_z_in(s, 3).wait_recv()
            w_s(3).start()
            for k in range(4):
                w_s_in(k).wait_recv()

        ps2[i] = project((h + 2) % 4).astype(BF16)
        x_copy(i, 0).start()
        x_copy(i, 1).start()
        pp[i] = project((h + 1) % 4).astype(BF16)
        x_copy(i, 2).start()
        pm[i] = project((h + 3) % 4).astype(BF16)
        x_copy(i, 3).start()

        @pl.when(i > 0)
        def _():
            merge(i - 1)

        po[i] = project(h)
        return m

    lax.fori_loop(0, 4, one, top(mx))
    merge(3)

    def finish(i, _):
        for k in range(2, 6):
            x_copy(i, k).wait_recv()
        total = po[i] + r2p[i].astype(F32) + r2m[i].astype(F32)
        out_ref[pl.ds(pl.multiple_of(i * 128, 128), 128), :] = jnp.transpose(total).astype(BF16)
        for k in range(6):
            x_copy(i, k).wait_send()
        return 0

    lax.fori_loop(0, 4, finish, 0)
    for kind in range(4):
        for part in range(2):
            kv(kind, part).wait_send()
    for s in range(4):
        if s < 3:
            w_y(s).wait_send()
        for k in range(4):
            w_z(s, k).wait_send()
        w_s(s).wait_send()


def local(query_rows, key_rows, value_rows, doc_blocks, out_weight):
    hbm = pl.BlockSpec(memory_space=pl.ANY)
    dma = pltpu.SemaphoreType.DMA
    return pl.pallas_call(
        kernel,
        out_shape=jax.ShapeDtypeStruct((512, 512), BF16),
        in_specs=[hbm, hbm, hbm, pl.BlockSpec(memory_space=pltpu.SMEM), hbm],
        out_specs=pl.BlockSpec(memory_space=pltpu.VMEM),
        scratch_shapes=[
            pltpu.VMEM((512, 1024), BF16),
            pltpu.VMEM((2560, 128), BF16),
            pltpu.VMEM((2560, 128), BF16),
            pltpu.VMEM((512, 128), BF16),
            pltpu.VMEM((128, 2560), BF16),
            pltpu.VMEM((4, 16, 128), BF16),
            pltpu.VMEM((4, 4, 2, 64, 1024), BF16),
            pltpu.VMEM((2, 2048, 256), F32),
            pltpu.VMEM((1024, 128), BF16),
            pltpu.VMEM((4, 512, 128), BF16),
            pltpu.VMEM((4, 512, 128), BF16),
            pltpu.VMEM((4, 512, 128), BF16),
            pltpu.VMEM((4, 512, 128), F32),
            pltpu.VMEM((4, 256, 128), BF16),
            pltpu.VMEM((4, 256, 128), BF16),
            pltpu.VMEM((4, 512, 128), BF16),
            pltpu.VMEM((4, 512, 128), BF16),
            dma((4,)),
            dma((4, 2)), dma((4, 2)),
            dma((3,)), dma((3,)),
            dma((4, 4)), dma((4, 4)),
            dma((4,)), dma((4,)),
            dma((4, 6)), dma((4, 6)),
        ],
        compiler_params=pltpu.CompilerParams(
            collective_id=0, has_side_effects=True, vmem_limit_bytes=48 * 2**20
        ),
    )(query_rows, key_rows, value_rows, doc_blocks, out_weight.T)


def solution(mesh):
    placed = (P("docs", "heads"), P("docs", "heads"), P("docs", "heads"), P(), P("heads", "docs"))
    return jax.shard_map(
        local, mesh=mesh, in_specs=placed, out_specs=P("docs", "heads"), check_vma=False
    )
```

```python
import functools
import math

import jax
import jax.numpy as jnp
from jax import lax
from jax.experimental import pallas as pl
from jax.experimental.pallas import tpu as pltpu
from jax.sharding import PartitionSpec as P

MESH = pl.DeviceIdType.MESH
NT = (((1,), (1,)), ((), ()))
NN = (((1,), (0,)), ((), ()))
F32, BF16 = jnp.float32, jnp.bfloat16
BIG = float(2**20)
SCALE = 128**-0.5 * math.log2(math.e)
CK = 512
NDOC = 16


def chunks(total):
    return [(o, min(CK, total - o)) for o in range(0, total, CK)]


def kernel(
    q_hbm, k_hbm, v_hbm, doc_ref, w_hbm, out_hbm,
    qv, kb, eb, vv, vb, bias, wb, s_buf, m_buf, a_buf, att,
    ps2, pp, pm, po, r1p, r1m, r2p, r2m, obuf,
    lsem, kvs, kvr, ws, wr, xs, xr,
):
    h, d = lax.axis_index("heads"), lax.axis_index("docs")
    c, y, z = d % 2, (d // 2) % 4, d // 8
    chip = d // 2

    def at(zz, yy):
        return (h, ((zz % 4) * 4 + yy % 4) * 2 + c)

    sib = (h, d + 1 - 2 * c)
    nxt = (h, ((chip + 1) % 16) * 2 + c)
    prv = (h, ((chip + 15) % 16) * 2 + c)
    yp, ym = at(z, y + 1), at(z, y + 3)
    zp, zm = at(z + 1, y), at(z + 3, y)
    xp, xm = ((h + 1) % 4, d), ((h + 3) % 4, d)

    lq = pltpu.make_async_copy(q_hbm, qv, lsem.at[0])
    lk = pltpu.make_async_copy(k_hbm, kb.at[pl.ds(2048, 512), :], lsem.at[1])
    lv = pltpu.make_async_copy(v_hbm, vv, lsem.at[2])
    lw = pltpu.make_async_copy(w_hbm, wb.at[z, y, c], lsem.at[3])
    lv.start()
    lk.start()
    lw.start()
    lq.start()

    barrier = pltpu.get_barrier_semaphore()
    for other in (sib, nxt, prv, yp, ym, zp, zm, xp, xm):
        pl.semaphore_signal(barrier, inc=1, device_id=other, device_id_type=MESH)

    def remote(src, dst, ss, rs, dev):
        return pltpu.make_async_remote_copy(
            src_ref=src, dst_ref=dst, send_sem=ss, recv_sem=rs, device_id=dev, device_id_type=MESH
        )

    def kv(kind, part):
        src = (4, 2, 4 - 2 * c, 2 - 2 * c)[kind]
        dst = (2, 0, 3, 1)[kind]
        dev = (nxt, nxt, sib, sib)[kind]
        if part == 0:
            a = kb.at[pl.ds(pl.multiple_of(src * 512, 512), 512), :]
            b = kb.at[pl.ds(dst * 512, 512), :]
        else:
            a = vb.at[:, pl.ds(pl.multiple_of(src * 512, 512), 512)]
            b = vb.at[:, pl.ds(dst * 512, 512)]
        return remote(a, b, kvs.at[kind, part], kvr.at[kind, part], dev)

    def w_ref(half, a, b):
        zz, yy = (z + b, y + a) if half == 0 else (z + a, y + b)
        return wb.at[zz % 4, yy % 4, c, pl.ds(32 * half, 32), :]

    def w_row(half, b, core):
        if half == 0:
            return wb.at[(z + b) % 4, :, core, pl.ds(0, 32), :]
        return wb.at[:, (y + b) % 4, core, pl.ds(32, 32), :]

    RING, OWN, FWD, PLUS, SHARE = range(5)

    def w_send(kind, half, s):
        if kind == SHARE:
            ref, dev = w_row(half, s, c), sib
        else:
            ref = w_ref(half, s, 1 if kind == FWD else 0)
            first, second, plus = (ym, zm, zp) if half == 0 else (zm, ym, yp)
            dev = (first, second, second, plus)[kind]
        return remote(ref, ref, ws.at[kind, half, s], wr.at[kind, half, s], dev)

    def w_come(kind, half, s):
        if kind == SHARE:
            ref = w_row(half, s, 1 - c)
        else:
            ref = w_ref(half, s + 1 if kind == RING else s, (0, 1, 2, 3)[kind])
        return remote(ref, ref, ws.at[kind, half, s], wr.at[kind, half, s], sib)

    def w_ring(s):
        for half in range(2):
            if s > 0:
                w_come(RING, half, s - 1).wait_recv()
            if s < 3:
                w_send(RING, half, s).start()
        for half in range(2):
            w_send(OWN, half, s).start()

    def w_fwd(s):
        for half in range(2):
            w_come(OWN, half, s).wait_recv()
            w_send(FWD, half, s).start()

    def w_share(b):
        for half in range(2):
            w_send(SHARE, half, b).start()

    lv.wait()
    vb[:, 2048:] = jnp.transpose(vv[...].astype(F32)).astype(BF16)

    lane = lax.broadcasted_iota(jnp.int32, (128, 128), 1)
    row = lax.broadcasted_iota(jnp.int32, (128, 128), 0)
    for w in range(20):
        eb[w * 128 : (w + 1) * 128, :] = (lane == w).astype(F32).astype(BF16)
    tri = jnp.where(row <= lane, 0.0, -BIG).astype(F32)
    tri2 = jnp.concatenate([tri, tri], axis=1)
    first_block = d * 4
    block = lax.broadcasted_iota(jnp.int32, (16, 128), 1) + (first_block - 16)
    doc = jnp.zeros((16, 128), jnp.int32)
    own = [jnp.int32(0)] * 4
    end = jnp.int32(0)
    for t in range(NDOC):
        end = end + doc_ref[t]
        doc = doc + (end <= block).astype(jnp.int32)
        own = [own[i] + (end <= first_block + i).astype(jnp.int32) for i in range(4)]
    for i in range(4):
        allowed = (doc == own[i]) & (block >= 0)
        bias[i] = jnp.where(allowed, 0.0, -BIG).astype(BF16)

    lk.wait()
    lw.wait()
    pl.semaphore_wait(barrier, 9)

    kv(0, 0).start()
    kv(0, 1).start()

    @pl.when(c == 0)
    def _():
        kv(2, 0).start()
        kv(2, 1).start()

    w_ring(0)
    lq.wait()

    def kv_near(part):
        kv(0, part).wait_recv()
        kv(1, part).start()

        @pl.when(c == 0)
        def _():
            kv(3, part).start()

        @pl.when(c == 1)
        def _():
            kv(2, part).start()

    def kv_far(part):
        kv(1, part).wait_recv()

        @pl.when(c == 1)
        def _():
            kv(3, part).start()

    w_ring(1)
    kv_near(0)
    w_fwd(0)
    kv_near(1)
    w_ring(2)
    kv(2, 0).wait_recv()
    kv(2, 1).wait_recv()

    def span(phase, i):
        return (1024, (9 + i) * 128) if phase == 0 else ((i + 1) * 128, (7 - i) * 128)

    def scores(phase, hp, i, slot, ck, mx):
        base, total = span(phase, i)
        o, n = chunks(total)[ck]
        q2 = qv[i * 128 : i * 128 + 128, pl.ds(pl.multiple_of(hp * 256, 256), 256)]
        b = jnp.concatenate([bias[i]] * 8, axis=0)
        qq = jnp.concatenate(
            [
                jnp.concatenate([q2[:, :128], b], axis=1),
                jnp.concatenate([q2[:, 128:], b], axis=1),
            ],
            axis=0,
        )
        rows = slice(base + o, base + o + n)
        kk = jnp.concatenate([kb[rows, :], eb[rows, :]], axis=1)
        s = lax.dot_general(kk, qq, NT, preferred_element_type=F32)
        if phase == 0 and o + n == total:
            last = s[n - 128 :] + tri2
            s = last if n == 128 else jnp.concatenate([s[: n - 128], last], axis=0)
        s_buf[slot, o : o + n, :] = s
        new = jnp.max(s.reshape(n // 8, 8, 256), axis=0)
        return new if mx is None else jnp.maximum(mx, new)

    def weigh(phase, i, slot, ck, m, acc):
        base, total = span(phase, i)
        o, n = chunks(total)[ck]
        s = s_buf[slot, o : o + n, :]
        p = jnp.exp2((s - m) * SCALE).astype(BF16)
        lhs = jnp.concatenate([vb[:, base + o : base + o + n], jnp.ones((16, n), BF16)], axis=0)
        t = lax.dot_general(lhs, p, NN, preferred_element_type=F32)
        return t if acc is None else acc + t

    def attention(phase, between):
        def top(hp, i, mx):
            m = jnp.max(mx, axis=0, keepdims=True)
            return m if phase == 0 else jnp.maximum(m, m_buf[hp, i, 0:1, :])

        def one(hp, m):
            for i in range(4):
                slot = i % 2
                nhp, ni = (hp, i + 1) if i < 3 else (jnp.minimum(hp + 1, 3), 0)
                mx, acc = None, None
                na, nb = len(chunks(span(phase, ni)[1])), len(chunks(span(phase, i)[1]))
                for ck in range(max(na, nb)):
                    if ck < na:
                        mx = scores(phase, nhp, ni, 1 - slot, ck, mx)
                    if ck < nb:
                        acc = weigh(phase, i, slot, ck, m, acc)
                if phase == 0:
                    m_buf[hp, i] = jnp.broadcast_to(m, (8, 256))
                    a_buf[hp, i] = acc[:136]
                else:
                    alpha = jnp.exp2((m_buf[hp, i, 0:1, :] - m) * SCALE)
                    acc = acc[:136] + a_buf[hp, i] * alpha
                    out = (acc[:128] / acc[128:129]).astype(BF16)
                    f = pl.multiple_of(hp * 256, 256)
                    att[pl.ds(f, 128), i * 128 : i * 128 + 128] = out[:, :128]
                    att[pl.ds(f + 128, 128), i * 128 : i * 128 + 128] = out[:, 128:]
                m = top(nhp, ni, mx)
            between(hp)
            return m

        mx = None
        for ck in range(len(chunks(span(phase, 0)[1]))):
            mx = scores(phase, 0, 0, 0, ck, mx)
        lax.fori_loop(0, 4, one, top(0, 0, mx))

    def first(hp):
        @pl.when(hp == 0)
        def _():
            w_fwd(1)

        @pl.when(hp == 1)
        def _():
            kv_far(0)
            w_ring(3)

        @pl.when(hp == 2)
        def _():
            w_share(0)
            w_fwd(2)

    attention(0, first)
    kv_far(1)
    for half in range(2):
        for s in range(4):
            w_send(PLUS, half, s).start()
    w_fwd(3)
    w_share(1)
    for part in range(2):
        kv(3, part).wait_recv()
    attention(1, lambda hp: None)

    for b in (2, 3):
        for half in range(2):
            for s in range(4):
                w_come((RING, OWN, FWD, PLUS)[b], half, s).wait_recv()
        w_share(b)
    for b in range(4):
        for half in range(2):
            w_come(SHARE, half, b).wait_recv()

    lo, hi = pl.ds(0, 256), pl.ds(256, 256)

    def x_copy(i, k):
        src, dst = (
            (ps2.at[i, lo], r1p.at[i]),
            (ps2.at[i, hi], r1m.at[i]),
            (pp.at[i, hi], r2p.at[i, hi]),
            (pm.at[i, lo], r2m.at[i, lo]),
            (pp.at[i, lo], r2p.at[i, lo]),
            (pm.at[i, hi], r2m.at[i, hi]),
        )[k]
        return remote(src, dst, xs.at[i, k], xr.at[i, k], (xp, xm)[k % 2])

    def project(j, into, kinds):
        w = wb[j].reshape(512, 1024)
        for pair in range(2):
            t = lax.dot_general(w, att[:, pair * 256 : pair * 256 + 256], NN, preferred_element_type=F32).astype(BF16)
            for u in range(2):
                into[2 * pair + u] = t[:, u * 128 : u * 128 + 128]
                for k in kinds:
                    x_copy(2 * pair + u, k).start()

    project((h + 2) % 4, ps2, (0, 1))
    project((h + 1) % 4, pp, (2,))
    project((h + 3) % 4, pm, (3,))
    project(h, po, ())

    def merge(i, _):
        x_copy(i, 0).wait_recv()
        pp[i, lo, :] = (pp[i, lo, :].astype(F32) + r1p[i].astype(F32)).astype(BF16)
        x_copy(i, 4).start()
        x_copy(i, 1).wait_recv()
        pm[i, hi, :] = (pm[i, hi, :].astype(F32) + r1m[i].astype(F32)).astype(BF16)
        x_copy(i, 5).start()
        return 0

    lax.fori_loop(0, 4, merge, 0)

    def write(i):
        return pltpu.make_async_copy(
            obuf.at[i], out_hbm.at[pl.ds(pl.multiple_of(i * 128, 128), 128), :], lsem.at[4 + i]
        )

    def finish(i, _):
        for k in range(2, 6):
            x_copy(i, k).wait_recv()
        total = po[i].astype(F32) + r2p[i].astype(F32) + r2m[i].astype(F32)
        obuf[i] = jnp.transpose(total).astype(BF16)
        write(i).start()
        for k in range(6):
            x_copy(i, k).wait_send()
        return 0

    lax.fori_loop(0, 4, finish, 0)
    for i in range(4):
        write(i).wait()
    for kind in range(4):
        for part in range(2):
            kv(kind, part).wait_send()
    for half in range(2):
        for kind in range(5):
            for s in range(3 if kind == RING else 4):
                w_send(kind, half, s).wait_send()


def local(query_rows, key_rows, value_rows, doc_blocks, out_weight):
    hbm = pl.BlockSpec(memory_space=pl.ANY)
    dma = pltpu.SemaphoreType.DMA
    return pl.pallas_call(
        kernel,
        out_shape=jax.ShapeDtypeStruct((512, 512), BF16),
        in_specs=[hbm, hbm, hbm, pl.BlockSpec(memory_space=pltpu.SMEM), hbm],
        out_specs=hbm,
        scratch_shapes=[
            pltpu.VMEM((512, 1024), BF16),
            pltpu.VMEM((2560, 128), BF16),
            pltpu.VMEM((2560, 128), BF16),
            pltpu.VMEM((512, 128), BF16),
            pltpu.VMEM((128, 2560), BF16),
            pltpu.VMEM((4, 16, 128), BF16),
            pltpu.VMEM((4, 4, 2, 64, 1024), BF16),
            pltpu.VMEM((2, 1536, 256), F32),
            pltpu.VMEM((4, 4, 8, 256), F32),
            pltpu.VMEM((4, 4, 136, 256), F32),
            pltpu.VMEM((1024, 512), BF16),
            pltpu.VMEM((4, 512, 128), BF16),
            pltpu.VMEM((4, 512, 128), BF16),
            pltpu.VMEM((4, 512, 128), BF16),
            pltpu.VMEM((4, 512, 128), BF16),
            pltpu.VMEM((4, 256, 128), BF16),
            pltpu.VMEM((4, 256, 128), BF16),
            pltpu.VMEM((4, 512, 128), BF16),
            pltpu.VMEM((4, 512, 128), BF16),
            pltpu.VMEM((4, 128, 512), BF16),
            dma((8,)),
            dma((4, 2)), dma((4, 2)),
            dma((5, 2, 4)), dma((5, 2, 4)),
            dma((4, 6)), dma((4, 6)),
        ],
        compiler_params=pltpu.CompilerParams(
            collective_id=0, has_side_effects=True, vmem_limit_bytes=62 * 2**20
        ),
    )(query_rows, key_rows, value_rows, doc_blocks, out_weight.T)


def solution(mesh):
    placed = (P("docs", "heads"), P("docs", "heads"), P("docs", "heads"), P(), P("heads", "docs"))
    return jax.shard_map(
        local, mesh=mesh, in_specs=placed, out_specs=P("docs", "heads"), check_vma=False
    )
```

```python
import functools
import math

import jax
import jax.numpy as jnp
from jax import lax
from jax.experimental import pallas as pl
from jax.experimental.pallas import tpu as pltpu
from jax.sharding import PartitionSpec as P

MESH = pl.DeviceIdType.MESH
NT = (((1,), (1,)), ((), ()))
NN = (((1,), (0,)), ((), ()))
F32, BF16 = jnp.float32, jnp.bfloat16
BIG = float(2**20)
SCALE = 128**-0.5 * math.log2(math.e)
CK = 512
NDOC = 16


def chunks(total):
    return [(o, min(CK, total - o)) for o in range(0, total, CK)]


def kernel(
    q_hbm, k_hbm, v_hbm, doc_ref, w_hbm, out_hbm,
    qv, kb, eb, vv, vb, bias, wb, s_buf, m_buf, a_buf, att,
    pb, r1p, r1m, r2p, r2m, obuf,
    lsem, kvs, kvr, ws, wr, xs, xr,
):
    h, d = lax.axis_index("heads"), lax.axis_index("docs")
    c, y, z = d % 2, (d // 2) % 4, d // 8
    chip = d // 2

    def at(zz, yy):
        return (h, ((zz % 4) * 4 + yy % 4) * 2 + c)

    sib = (h, d + 1 - 2 * c)
    nxt = (h, ((chip + 1) % 16) * 2 + c)
    prv = (h, ((chip + 15) % 16) * 2 + c)
    yp, ym = at(z, y + 1), at(z, y + 3)
    zp, zm = at(z + 1, y), at(z + 3, y)
    xp, xm = ((h + 1) % 4, d), ((h + 3) % 4, d)

    lq = pltpu.make_async_copy(q_hbm, qv, lsem.at[0])
    lk = pltpu.make_async_copy(k_hbm, kb.at[pl.ds(2048, 512), :], lsem.at[1])
    lv = pltpu.make_async_copy(v_hbm, vv, lsem.at[2])
    lw = pltpu.make_async_copy(w_hbm, wb.at[z, y, c], lsem.at[3])
    lv.start()
    lk.start()
    lw.start()
    lq.start()

    barrier = pltpu.get_barrier_semaphore()
    for other in (sib, nxt, prv, yp, ym, zp, zm, xp, xm):
        pl.semaphore_signal(barrier, inc=1, device_id=other, device_id_type=MESH)

    def remote(src, dst, ss, rs, dev):
        return pltpu.make_async_remote_copy(
            src_ref=src, dst_ref=dst, send_sem=ss, recv_sem=rs, device_id=dev, device_id_type=MESH
        )

    def kv(kind, part):
        src = (4, 2, 4 - 2 * c, 2 - 2 * c)[kind]
        dst = (2, 0, 3, 1)[kind]
        dev = (nxt, nxt, sib, sib)[kind]
        if part == 0:
            a = kb.at[pl.ds(pl.multiple_of(src * 512, 512), 512), :]
            b = kb.at[pl.ds(dst * 512, 512), :]
        else:
            a = vb.at[:, pl.ds(pl.multiple_of(src * 512, 512), 512)]
            b = vb.at[:, pl.ds(dst * 512, 512)]
        return remote(a, b, kvs.at[kind, part], kvr.at[kind, part], dev)

    def w_ref(a, b, core):
        return wb.at[(z + a) % 4, (y + b) % 4, core]

    RING, OWN, FWD, PLUS, SHARE = 0, 1, 2, 3, 4

    def w_send(kind, s):
        if kind == RING:
            ref, dev = w_ref(s, 0, c), zm
        elif kind >= SHARE:
            ref, dev = w_ref(s, kind - SHARE, c), sib
        elif kind == OWN or s == 0 or (kind == PLUS and s == 2):
            ref = w_ref(s, 1 if kind == FWD else 0, c)
            dev = yp if kind == PLUS else ym
        else:
            ref = w_ref(1 if s == 2 else 0, kind, c)
            dev = zp if s == 3 else zm
        return remote(ref, ref, ws.at[kind, s], wr.at[kind, s], dev)

    def w_come(kind, s):
        if kind == RING:
            ref = w_ref(s + 1, 0, c)
        elif kind >= SHARE:
            ref = w_ref(s, kind - SHARE, 1 - c)
        else:
            ref = w_ref(s, (0, 1, 2, 3)[kind], c)
        return remote(ref, ref, ws.at[kind, s], wr.at[kind, s], sib)

    def w_own(s):
        w_send(OWN, s).start()
        w_send(SHARE, s).start()

    def w_fwd(s):
        w_come(OWN, s).wait_recv()
        if s == 0:
            w_send(FWD, 0).start()
        w_send(SHARE + 1, s).start()

    def w_ring(s):
        w_come(RING, s - 1).wait_recv()
        if s < 3:
            w_send(RING, s).start()
        w_own(s)

    lv.wait()
    vb[:, 2048:] = jnp.transpose(vv[...].astype(F32)).astype(BF16)

    lane = lax.broadcasted_iota(jnp.int32, (128, 128), 1)
    row = lax.broadcasted_iota(jnp.int32, (128, 128), 0)
    for w in range(20):
        eb[w * 128 : (w + 1) * 128, :] = (lane == w).astype(F32).astype(BF16)
    tri = jnp.where(row <= lane, 0.0, -BIG).astype(F32)
    tri2 = jnp.concatenate([tri, tri], axis=1)
    first_block = d * 4
    block = lax.broadcasted_iota(jnp.int32, (16, 128), 1) + (first_block - 16)
    doc = jnp.zeros((16, 128), jnp.int32)
    own = [jnp.int32(0)] * 4
    end = jnp.int32(0)
    for t in range(NDOC):
        end = end + doc_ref[t]
        doc = doc + (end <= block).astype(jnp.int32)
        own = [own[i] + (end <= first_block + i).astype(jnp.int32) for i in range(4)]
    for i in range(4):
        allowed = (doc == own[i]) & (block >= 0)
        bias[i] = jnp.where(allowed, 0.0, -BIG).astype(BF16)

    lk.wait()
    lw.wait()
    pl.semaphore_wait(barrier, 9)

    kv(0, 0).start()
    kv(0, 1).start()

    @pl.when(c == 0)
    def _():
        kv(2, 0).start()
        kv(2, 1).start()

    w_send(RING, 0).start()
    w_own(0)
    lq.wait()

    def kv_near(part):
        kv(0, part).wait_recv()
        kv(1, part).start()

        @pl.when(c == 0)
        def _():
            kv(3, part).start()

        @pl.when(c == 1)
        def _():
            kv(2, part).start()

    def kv_far(part):
        kv(1, part).wait_recv()

        @pl.when(c == 1)
        def _():
            kv(3, part).start()

    def span(phase, i):
        return ((2048, (i + 1) * 128), (1024, 1024), ((i + 1) * 128, (7 - i) * 128))[phase]

    def scores(phase, hp, i, slot, ck, mx):
        base, total = span(phase, i)
        o, n = chunks(total)[ck]
        q2 = qv[i * 128 : i * 128 + 128, pl.ds(pl.multiple_of(hp * 256, 256), 256)]
        b = jnp.concatenate([bias[i]] * 8, axis=0)
        qq = jnp.concatenate(
            [
                jnp.concatenate([q2[:, :128], b], axis=1),
                jnp.concatenate([q2[:, 128:], b], axis=1),
            ],
            axis=0,
        )
        rows = slice(base + o, base + o + n)
        kk = jnp.concatenate([kb[rows, :], eb[rows, :]], axis=1)
        s = lax.dot_general(kk, qq, NT, preferred_element_type=F32)
        if phase == 0 and o + n == total:
            last = s[n - 128 :] + tri2
            s = last if n == 128 else jnp.concatenate([s[: n - 128], last], axis=0)
        s_buf[slot, o : o + n, :] = s
        new = jnp.max(s.reshape(n // 8, 8, 256), axis=0)
        return new if mx is None else jnp.maximum(mx, new)

    def weigh(phase, i, slot, ck, m, acc):
        base, total = span(phase, i)
        o, n = chunks(total)[ck]
        s = s_buf[slot, o : o + n, :]
        p = jnp.exp2((s - m) * SCALE).astype(BF16)
        lhs = jnp.concatenate([vb[:, base + o : base + o + n], jnp.ones((16, n), BF16)], axis=0)
        t = lax.dot_general(lhs, p, NN, preferred_element_type=F32)
        return t if acc is None else acc + t

    def attention(phase, between):
        def top(hp, i, mx):
            m = jnp.max(mx, axis=0, keepdims=True)
            return m if phase == 0 else jnp.maximum(m, m_buf[hp, i, 0:1, :])

        def one(hp, m):
            for i in range(4):
                slot = i % 2
                nhp, ni = (hp, i + 1) if i < 3 else (jnp.minimum(hp + 1, 3), 0)
                mx, acc = None, None
                na, nb = len(chunks(span(phase, ni)[1])), len(chunks(span(phase, i)[1]))
                for ck in range(max(na, nb)):
                    if ck < na:
                        mx = scores(phase, nhp, ni, 1 - slot, ck, mx)
                    if ck < nb:
                        acc = weigh(phase, i, slot, ck, m, acc)
                acc = acc[:136]
                if phase > 0:
                    alpha = jnp.exp2((m_buf[hp, i, 0:1, :] - m) * SCALE)
                    acc = acc + a_buf[hp, i] * alpha
                if phase < 2:
                    m_buf[hp, i] = jnp.broadcast_to(m, (8, 256))
                    a_buf[hp, i] = acc
                else:
                    out = (acc[:128] / acc[128:129]).astype(BF16)
                    f = pl.multiple_of(hp * 256, 256)
                    att[pl.ds(f, 128), i * 128 : i * 128 + 128] = out[:, :128]
                    att[pl.ds(f + 128, 128), i * 128 : i * 128 + 128] = out[:, 128:]
                m = top(nhp, ni, mx)
            between(hp)
            return m

        mx = None
        for ck in range(len(chunks(span(phase, 0)[1]))):
            mx = scores(phase, 0, 0, 0, ck, mx)
        lax.fori_loop(0, 4, one, top(0, 0, mx))

    attention(0, lambda hp: None)
    w_ring(1)
    kv_near(0)
    kv_near(1)
    w_ring(2)
    w_fwd(0)
    kv(2, 0).wait_recv()
    kv(2, 1).wait_recv()

    def first(hp):
        @pl.when(hp == 0)
        def _():
            w_fwd(1)

        @pl.when(hp == 1)
        def _():
            w_ring(3)

        @pl.when(hp == 2)
        def _():
            kv_far(0)
            w_fwd(2)
            w_come(FWD, 0).wait_recv()
            w_send(FWD, 1).start()
            w_send(SHARE + FWD, 0).start()

    def second(hp):
        @pl.when(hp == 0)
        def _():
            w_fwd(3)

        @pl.when(hp == 1)
        def _():
            w_come(FWD, 1).wait_recv()
            w_send(FWD, 2).start()
            w_send(SHARE + FWD, 1).start()

        @pl.when(hp == 2)
        def _():
            w_come(PLUS, 0).wait_recv()
            w_send(PLUS, 1).start()
            w_send(PLUS, 3).start()
            w_send(PLUS, 2).start()
            w_send(SHARE + PLUS, 0).start()

    attention(1, first)
    kv_far(1)
    w_send(PLUS, 0).start()
    w_send(FWD, 3).start()
    for part in range(2):
        kv(3, part).wait_recv()
    attention(2, second)

    lo, hi = pl.ds(0, 64), pl.ds(64, 64)
    left, right, far = (h + 3) % 4, (h + 1) % 4, (h + 2) % 4

    def x_copy(g, k):
        src, dst = (
            (pb.at[g, far, lo], r1p.at[g]),
            (pb.at[g, far, hi], r1m.at[g]),
            (pb.at[g, right, hi], r2p.at[g, hi]),
            (pb.at[g, left, lo], r2m.at[g, lo]),
            (pb.at[g, right, lo], r2p.at[g, lo]),
            (pb.at[g, left, hi], r2m.at[g, hi]),
        )[k]
        return remote(src, dst, xs.at[g, k], xr.at[g, k], (xp, xm)[k % 2])

    def project(b):
        for s in range(4):
            w_come(SHARE + b, s).wait_recv()
        g = (y + b) % 4
        w = wb[:, g].reshape(512, 1024)
        for half in range(2):
            cols = slice(half * 256, half * 256 + 256)
            t = lax.dot_general(w, att[:, cols], NN, preferred_element_type=F32).astype(BF16)
            pb[g, :, :, cols] = t.reshape(4, 128, 256)
        for k in range(4):
            x_copy(g, k).start()

    def merge(b):
        g = (y + b) % 4
        x_copy(g, 0).wait_recv()
        pb[g, right, lo, :] = (pb[g, right, lo, :].astype(F32) + r1p[g].astype(F32)).astype(BF16)
        x_copy(g, 4).start()
        x_copy(g, 1).wait_recv()
        pb[g, left, hi, :] = (pb[g, left, hi, :].astype(F32) + r1m[g].astype(F32)).astype(BF16)
        x_copy(g, 5).start()

    def write(g):
        return pltpu.make_async_copy(
            obuf.at[g], out_hbm.at[:, pl.ds(pl.multiple_of(g * 128, 128), 128)], lsem.at[4 + g]
        )

    def finish(b):
        g = (y + b) % 4
        for k in range(2, 6):
            x_copy(g, k).wait_recv()
        total = pb[g, h].astype(F32) + r2p[g].astype(F32) + r2m[g].astype(F32)
        obuf[g] = jnp.transpose(total).astype(BF16)
        write(g).start()

    def w_last(kind, steps):
        for s in steps:
            w_come(kind, s).wait_recv()
            w_send(SHARE + kind, s).start()

    project(0)
    project(1)
    merge(0)
    merge(1)
    w_last(FWD, (3, 2))
    project(2)
    w_last(PLUS, (1, 3, 2))
    project(3)
    finish(0)
    merge(2)
    finish(1)
    merge(3)
    for kind in range(4):
        for part in range(2):
            kv(kind, part).wait_send()
    for kind in range(SHARE + 4):
        for s in range(3 if kind == RING else 4):
            w_send(kind, s).wait_send()
    finish(2)
    for g in range(3):
        for k in range(4):
            x_copy((y + g) % 4, k).wait_send()
    finish(3)
    for g in range(4):
        write(g).wait()
    for b in range(4):
        for k in range(4 if b < 3 else 0, 6):
            x_copy((y + b) % 4, k).wait_send()


def local(query_rows, key_rows, value_rows, doc_blocks, out_weight):
    hbm = pl.BlockSpec(memory_space=pl.ANY)
    dma = pltpu.SemaphoreType.DMA
    return pl.pallas_call(
        kernel,
        out_shape=jax.ShapeDtypeStruct((512, 512), BF16),
        in_specs=[hbm, hbm, hbm, pl.BlockSpec(memory_space=pltpu.SMEM), hbm],
        out_specs=hbm,
        scratch_shapes=[
            pltpu.VMEM((512, 1024), BF16),
            pltpu.VMEM((2560, 128), BF16),
            pltpu.VMEM((2560, 128), BF16),
            pltpu.VMEM((512, 128), BF16),
            pltpu.VMEM((128, 2560), BF16),
            pltpu.VMEM((4, 16, 128), BF16),
            pltpu.VMEM((4, 4, 2, 64, 1024), BF16),
            pltpu.VMEM((2, 1024, 256), F32),
            pltpu.VMEM((4, 4, 8, 256), F32),
            pltpu.VMEM((4, 4, 136, 256), F32),
            pltpu.VMEM((1024, 512), BF16),
            pltpu.VMEM((4, 4, 128, 512), BF16),
            pltpu.VMEM((4, 64, 512), BF16),
            pltpu.VMEM((4, 64, 512), BF16),
            pltpu.VMEM((4, 128, 512), BF16),
            pltpu.VMEM((4, 128, 512), BF16),
            pltpu.VMEM((4, 512, 128), BF16),
            dma((8,)),
            dma((4, 2)), dma((4, 2)),
            dma((8, 4)), dma((8, 4)),
            dma((4, 6)), dma((4, 6)),
        ],
        compiler_params=pltpu.CompilerParams(
            collective_id=0, has_side_effects=True, vmem_limit_bytes=62 * 2**20
        ),
    )(query_rows, key_rows, value_rows, doc_blocks, out_weight.T)


def solution(mesh):
    placed = (P("docs", "heads"), P("docs", "heads"), P("docs", "heads"), P(), P("heads", "docs"))
    return jax.shard_map(
        local, mesh=mesh, in_specs=placed, out_specs=P("docs", "heads"), check_vma=False
    )
```

```python
import functools
import math

import jax
import jax.numpy as jnp
from jax import lax
from jax.experimental import pallas as pl
from jax.experimental.pallas import tpu as pltpu
from jax.sharding import PartitionSpec as P

MESH = pl.DeviceIdType.MESH
NT = (((1,), (1,)), ((), ()))
NN = (((1,), (0,)), ((), ()))
F32, BF16 = jnp.float32, jnp.bfloat16
BIG = float(2**20)
SCALE = 128**-0.5 * math.log2(math.e)
CK = 512
NDOC = 16


def chunks(total):
    return [(o, min(CK, total - o)) for o in range(0, total, CK)]


def kernel(
    q_hbm, k_hbm, v_hbm, doc_ref, w_hbm, out_hbm,
    qv, kb, eb, vv, vb, bias, wb, s_buf, m_buf, a_buf, att,
    pb, r1p, r1m, r2p, r2m, obuf,
    lsem, kvs, kvr, ws, wr, xs, xr,
):
    h, d = lax.axis_index("heads"), lax.axis_index("docs")
    c, y, z = d % 2, (d // 2) % 4, d // 8
    chip = d // 2

    def at(zz, yy):
        return (h, ((zz % 4) * 4 + yy % 4) * 2 + c)

    sib = (h, d + 1 - 2 * c)
    nxt = (h, ((chip + 1) % 16) * 2 + c)
    prv = (h, ((chip + 15) % 16) * 2 + c)
    yp, ym = at(z, y + 1), at(z, y + 3)
    zp, zm = at(z + 1, y), at(z + 3, y)
    xp, xm = ((h + 1) % 4, d), ((h + 3) % 4, d)

    lq = pltpu.make_async_copy(q_hbm, qv, lsem.at[0])
    lk = pltpu.make_async_copy(k_hbm, kb.at[pl.ds(2048, 512), :], lsem.at[1])
    lv = pltpu.make_async_copy(v_hbm, vv, lsem.at[2])
    lw = pltpu.make_async_copy(w_hbm, wb.at[z, y, c], lsem.at[3])
    lv.start()
    lk.start()
    lw.start()
    lq.start()

    barrier = pltpu.get_barrier_semaphore()
    for other in (sib, nxt, prv, yp, ym, zp, zm, xp, xm):
        pl.semaphore_signal(barrier, inc=1, device_id=other, device_id_type=MESH)

    def remote(src, dst, ss, rs, dev):
        return pltpu.make_async_remote_copy(
            src_ref=src, dst_ref=dst, send_sem=ss, recv_sem=rs, device_id=dev, device_id_type=MESH
        )

    def kv(kind, part):
        src = (4, 2, 4 - 2 * c, 2 - 2 * c)[kind]
        dst = (2, 0, 3, 1)[kind]
        dev = (nxt, nxt, sib, sib)[kind]
        if part == 0:
            a = kb.at[pl.ds(pl.multiple_of(src * 512, 512), 512), :]
            b = kb.at[pl.ds(dst * 512, 512), :]
        else:
            a = vb.at[:, pl.ds(pl.multiple_of(src * 512, 512), 512)]
            b = vb.at[:, pl.ds(dst * 512, 512)]
        return remote(a, b, kvs.at[kind, part], kvr.at[kind, part], dev)

    def w_ref(a, b, core):
        return wb.at[(z + a) % 4, (y + b) % 4, core]

    RING, OWN, FWD, PLUS, SHARE = 0, 1, 2, 3, 4

    def w_send(kind, s):
        if kind == RING:
            ref, dev = w_ref(s, 0, c), zm
        elif kind >= SHARE:
            ref, dev = w_ref(s, kind - SHARE, c), sib
        elif kind == OWN or s == 0 or (kind == PLUS and s == 2):
            ref = w_ref(s, 1 if kind == FWD else 0, c)
            dev = yp if kind == PLUS else ym
        else:
            ref = w_ref(1 if s == 2 else 0, kind, c)
            dev = zp if s == 3 else zm
        return remote(ref, ref, ws.at[kind, s], wr.at[kind, s], dev)

    def w_come(kind, s):
        if kind == RING:
            ref = w_ref(s + 1, 0, c)
        elif kind >= SHARE:
            ref = w_ref(s, kind - SHARE, 1 - c)
        else:
            ref = w_ref(s, (0, 1, 2, 3)[kind], c)
        return remote(ref, ref, ws.at[kind, s], wr.at[kind, s], sib)

    def w_own(s):
        w_send(OWN, s).start()
        w_send(SHARE, s).start()

    def w_fwd(s):
        w_come(OWN, s).wait_recv()
        if s == 0:
            w_send(FWD, 0).start()
        w_send(SHARE + 1, s).start()

    def w_ring(s):
        w_come(RING, s - 1).wait_recv()
        if s < 3:
            w_send(RING, s).start()
        w_own(s)

    lv.wait()
    vb[:, 2048:] = jnp.transpose(vv[...].astype(F32)).astype(BF16)

    lane = lax.broadcasted_iota(jnp.int32, (128, 128), 1)
    row = lax.broadcasted_iota(jnp.int32, (128, 128), 0)
    for w in range(20):
        eb[w * 128 : (w + 1) * 128, :] = (lane == w).astype(F32).astype(BF16)
    tri = jnp.where(row <= lane, 0.0, -BIG).astype(F32)
    tri2 = jnp.concatenate([tri, tri], axis=1)
    first_block = d * 4
    block = lax.broadcasted_iota(jnp.int32, (16, 128), 1) + (first_block - 16)
    doc = jnp.zeros((16, 128), jnp.int32)
    own = [jnp.int32(0)] * 4
    end = jnp.int32(0)
    for t in range(NDOC):
        end = end + doc_ref[t]
        doc = doc + (end <= block).astype(jnp.int32)
        own = [own[i] + (end <= first_block + i).astype(jnp.int32) for i in range(4)]
    for i in range(4):
        allowed = (doc == own[i]) & (block >= 0)
        bias[i] = jnp.where(allowed, 0.0, -BIG).astype(BF16)

    lk.wait()
    lw.wait()
    pl.semaphore_wait(barrier, 9)

    kv(0, 0).start()
    kv(0, 1).start()

    @pl.when(c == 0)
    def _():
        kv(2, 0).start()
        kv(2, 1).start()

    w_send(RING, 0).start()
    w_own(0)
    lq.wait()

    def kv_near(part):
        kv(0, part).wait_recv()
        kv(1, part).start()

        @pl.when(c == 0)
        def _():
            kv(3, part).start()

        @pl.when(c == 1)
        def _():
            kv(2, part).start()

    def kv_far(part):
        kv(1, part).wait_recv()

        @pl.when(c == 1)
        def _():
            kv(3, part).start()

    def span(phase, i):
        return ((2048, (i + 1) * 128), (1024, 1024), ((i + 1) * 128, (7 - i) * 128))[phase]

    def scores(phase, hp, i, slot, ck, mx):
        base, total = span(phase, i)
        o, n = chunks(total)[ck]
        q2 = qv[i * 128 : i * 128 + 128, pl.ds(pl.multiple_of(hp * 256, 256), 256)]
        b = jnp.concatenate([bias[i]] * 8, axis=0)
        qq = jnp.concatenate(
            [
                jnp.concatenate([q2[:, :128], b], axis=1),
                jnp.concatenate([q2[:, 128:], b], axis=1),
            ],
            axis=0,
        )
        rows = slice(base + o, base + o + n)
        kk = jnp.concatenate([kb[rows, :], eb[rows, :]], axis=1)
        s = lax.dot_general(kk, qq, NT, preferred_element_type=F32)
        if phase == 0 and o + n == total:
            last = s[n - 128 :] + tri2
            s = last if n == 128 else jnp.concatenate([s[: n - 128], last], axis=0)
        s_buf[slot, o : o + n, :] = s
        new = jnp.max(s.reshape(n // 8, 8, 256), axis=0)
        return new if mx is None else jnp.maximum(mx, new)

    def weigh(phase, i, slot, ck, m, acc):
        base, total = span(phase, i)
        o, n = chunks(total)[ck]
        s = s_buf[slot, o : o + n, :]
        p = jnp.exp2((s - m) * SCALE).astype(BF16)
        lhs = jnp.concatenate([vb[:, base + o : base + o + n], jnp.ones((16, n), BF16)], axis=0)
        t = lax.dot_general(lhs, p, NN, preferred_element_type=F32)
        return t if acc is None else acc + t

    def attention(phase, between):
        def top(hp, i, mx):
            m = jnp.max(mx, axis=0, keepdims=True)
            return m if phase == 0 else jnp.maximum(m, m_buf[hp, i, 0:1, :])

        def one(hp, m):
            for i in range(4):
                slot = i % 2
                nhp, ni = (hp, i + 1) if i < 3 else (jnp.minimum(hp + 1, 3), 0)
                mx, acc = None, None
                na, nb = len(chunks(span(phase, ni)[1])), len(chunks(span(phase, i)[1]))
                for ck in range(max(na, nb)):
                    if ck < na:
                        mx = scores(phase, nhp, ni, 1 - slot, ck, mx)
                    if ck < nb:
                        acc = weigh(phase, i, slot, ck, m, acc)
                acc = acc[:136]
                if phase > 0:
                    alpha = jnp.exp2((m_buf[hp, i, 0:1, :] - m) * SCALE)
                    acc = acc + a_buf[hp, i] * alpha
                if phase < 2:
                    m_buf[hp, i] = jnp.broadcast_to(m, (8, 256))
                    a_buf[hp, i] = acc
                else:
                    out = (acc[:128] / acc[128:129]).astype(BF16)
                    f = pl.multiple_of(hp * 256, 256)
                    att[pl.ds(f, 128), i * 128 : i * 128 + 128] = out[:, :128]
                    att[pl.ds(f + 128, 128), i * 128 : i * 128 + 128] = out[:, 128:]
                m = top(nhp, ni, mx)
            between(hp)
            return m

        mx = None
        for ck in range(len(chunks(span(phase, 0)[1]))):
            mx = scores(phase, 0, 0, 0, ck, mx)
        lax.fori_loop(0, 4, one, top(0, 0, mx))

    attention(0, lambda hp: None)
    w_ring(1)
    kv_near(0)
    kv_near(1)
    w_ring(2)
    w_fwd(0)
    kv(2, 0).wait_recv()
    kv(2, 1).wait_recv()

    def first(hp):
        @pl.when(hp == 0)
        def _():
            w_fwd(1)

        @pl.when(hp == 1)
        def _():
            w_ring(3)

        @pl.when(hp == 2)
        def _():
            kv_far(0)
            w_fwd(2)
            w_come(FWD, 0).wait_recv()
            w_send(FWD, 1).start()
            w_send(SHARE + FWD, 0).start()

    def second(hp):
        @pl.when(hp == 0)
        def _():
            w_fwd(3)

        @pl.when(hp == 1)
        def _():
            w_come(FWD, 1).wait_recv()
            w_send(FWD, 2).start()
            w_send(SHARE + FWD, 1).start()

        @pl.when(hp == 2)
        def _():
            w_come(PLUS, 0).wait_recv()
            w_send(PLUS, 1).start()
            w_send(PLUS, 3).start()
            w_send(PLUS, 2).start()
            w_send(SHARE + PLUS, 0).start()

    attention(1, first)
    kv_far(1)
    w_send(PLUS, 0).start()
    w_send(FWD, 3).start()
    for part in range(2):
        kv(3, part).wait_recv()
    attention(2, second)

    lo, hi = pl.ds(0, 64), pl.ds(64, 64)
    left, right, far = (h + 3) % 4, (h + 1) % 4, (h + 2) % 4

    def x_copy(g, k):
        src, dst = (
            (pb.at[g, far, lo], r1p.at[g]),
            (pb.at[g, far, hi], r1m.at[g]),
            (pb.at[g, right, hi], r2p.at[g, hi]),
            (pb.at[g, left, lo], r2m.at[g, lo]),
            (pb.at[g, right, lo], r2p.at[g, lo]),
            (pb.at[g, left, hi], r2m.at[g, hi]),
        )[k]
        return remote(src, dst, xs.at[g, k], xr.at[g, k], (xp, xm)[k % 2])

    def project(b):
        for s in range(4):
            w_come(SHARE + b, s).wait_recv()
        g = (y + b) % 4
        w = wb[:, g].reshape(512, 1024)
        for half in range(2):
            cols = slice(half * 256, half * 256 + 256)
            t = lax.dot_general(w, att[:, cols], NN, preferred_element_type=F32).astype(BF16)
            pb[g, :, :, cols] = t.reshape(4, 128, 256)
        for k in range(4):
            x_copy(g, k).start()

    def merge(b):
        g = (y + b) % 4
        x_copy(g, 0).wait_recv()
        pb[g, right, lo, :] = (pb[g, right, lo, :].astype(F32) + r1p[g].astype(F32)).astype(BF16)
        x_copy(g, 4).start()
        x_copy(g, 1).wait_recv()
        pb[g, left, hi, :] = (pb[g, left, hi, :].astype(F32) + r1m[g].astype(F32)).astype(BF16)
        x_copy(g, 5).start()

    def write(g):
        return pltpu.make_async_copy(
            obuf.at[g], out_hbm.at[:, pl.ds(pl.multiple_of(g * 128, 128), 128)], lsem.at[4 + g]
        )

    def finish(b):
        g = (y + b) % 4
        for k in range(2, 6):
            x_copy(g, k).wait_recv()
        total = pb[g, h].astype(F32) + r2p[g].astype(F32) + r2m[g].astype(F32)
        obuf[g] = jnp.transpose(total).astype(BF16)
        write(g).start()

    def w_last(kind, steps):
        for s in steps:
            w_come(kind, s).wait_recv()
            w_send(SHARE + kind, s).start()

    project(0)
    project(1)
    w_last(FWD, (3, 2))
    w_last(PLUS, (1, 3, 2))
    merge(0)
    merge(1)
    project(2)
    project(3)
    finish(0)
    merge(2)
    finish(1)
    merge(3)
    for kind in range(4):
        for part in range(2):
            kv(kind, part).wait_send()
    for kind in range(SHARE + 4):
        for s in range(3 if kind == RING else 4):
            w_send(kind, s).wait_send()
    finish(2)
    for g in range(3):
        for k in range(4):
            x_copy((y + g) % 4, k).wait_send()
    finish(3)
    for g in range(4):
        write(g).wait()
    for b in range(4):
        for k in range(4 if b < 3 else 0, 6):
            x_copy((y + b) % 4, k).wait_send()


def local(query_rows, key_rows, value_rows, doc_blocks, out_weight):
    hbm = pl.BlockSpec(memory_space=pl.ANY)
    dma = pltpu.SemaphoreType.DMA
    return pl.pallas_call(
        kernel,
        out_shape=jax.ShapeDtypeStruct((512, 512), BF16),
        in_specs=[hbm, hbm, hbm, pl.BlockSpec(memory_space=pltpu.SMEM), hbm],
        out_specs=hbm,
        scratch_shapes=[
            pltpu.VMEM((512, 1024), BF16),
            pltpu.VMEM((2560, 128), BF16),
            pltpu.VMEM((2560, 128), BF16),
            pltpu.VMEM((512, 128), BF16),
            pltpu.VMEM((128, 2560), BF16),
            pltpu.VMEM((4, 16, 128), BF16),
            pltpu.VMEM((4, 4, 2, 64, 1024), BF16),
            pltpu.VMEM((2, 1024, 256), F32),
            pltpu.VMEM((4, 4, 8, 256), F32),
            pltpu.VMEM((4, 4, 136, 256), F32),
            pltpu.VMEM((1024, 512), BF16),
            pltpu.VMEM((4, 4, 128, 512), BF16),
            pltpu.VMEM((4, 64, 512), BF16),
            pltpu.VMEM((4, 64, 512), BF16),
            pltpu.VMEM((4, 128, 512), BF16),
            pltpu.VMEM((4, 128, 512), BF16),
            pltpu.VMEM((4, 512, 128), BF16),
            dma((8,)),
            dma((4, 2)), dma((4, 2)),
            dma((8, 4)), dma((8, 4)),
            dma((4, 6)), dma((4, 6)),
        ],
        compiler_params=pltpu.CompilerParams(
            collective_id=0, has_side_effects=True, vmem_limit_bytes=62 * 2**20
        ),
    )(query_rows, key_rows, value_rows, doc_blocks, out_weight.T)


def solution(mesh):
    placed = (P("docs", "heads"), P("docs", "heads"), P("docs", "heads"), P(), P("heads", "docs"))
    return jax.shard_map(
        local, mesh=mesh, in_specs=placed, out_specs=P("docs", "heads"), check_vma=False
    )
```

```python
import functools
import math

import jax
import jax.numpy as jnp
from jax import lax
from jax.experimental import pallas as pl
from jax.experimental.pallas import tpu as pltpu
from jax.sharding import PartitionSpec as P

MESH = pl.DeviceIdType.MESH
NT = (((1,), (1,)), ((), ()))
NN = (((1,), (0,)), ((), ()))
F32, BF16 = jnp.float32, jnp.bfloat16
BIG = float(2**20)
SCALE = 128**-0.5 * math.log2(math.e)
CK = 512
NDOC = 16


def chunks(total):
    return [(o, min(CK, total - o)) for o in range(0, total, CK)]


def kernel(
    q_hbm, k_hbm, v_hbm, doc_ref, w_hbm, out_hbm,
    qv, kb, eb, vv, vb, bias, wb, s_buf, m_buf, a_buf, att,
    pb, r1p, r1m, r2p, r2m, obuf,
    lsem, kvs, kvr, ws, wr, xs, xr,
):
    h, d = lax.axis_index("heads"), lax.axis_index("docs")
    c, y, z = d % 2, (d // 2) % 4, d // 8
    chip = d // 2

    def at(zz, yy):
        return (h, ((zz % 4) * 4 + yy % 4) * 2 + c)

    sib = (h, d + 1 - 2 * c)
    nxt = (h, ((chip + 1) % 16) * 2 + c)
    prv = (h, ((chip + 15) % 16) * 2 + c)
    yp, ym = at(z, y + 1), at(z, y + 3)
    zp, zm = at(z + 1, y), at(z + 3, y)
    xp, xm = ((h + 1) % 4, d), ((h + 3) % 4, d)

    lq = pltpu.make_async_copy(q_hbm, qv, lsem.at[0])
    lk = pltpu.make_async_copy(k_hbm, kb.at[pl.ds(2048, 512), :], lsem.at[1])
    lv = pltpu.make_async_copy(v_hbm, vv, lsem.at[2])
    lw = pltpu.make_async_copy(w_hbm, wb.at[z, y, c], lsem.at[3])
    lv.start()
    lk.start()
    lw.start()
    lq.start()

    barrier = pltpu.get_barrier_semaphore()
    for other in (sib, nxt, prv, yp, ym, zp, zm, xp, xm):
        pl.semaphore_signal(barrier, inc=1, device_id=other, device_id_type=MESH)

    def remote(src, dst, ss, rs, dev):
        return pltpu.make_async_remote_copy(
            src_ref=src, dst_ref=dst, send_sem=ss, recv_sem=rs, device_id=dev, device_id_type=MESH
        )

    def kv(kind, part):
        src = (4, 2, 4 - 2 * c, 2 - 2 * c)[kind]
        dst = (2, 0, 3, 1)[kind]
        dev = (nxt, nxt, sib, sib)[kind]
        if part == 0:
            a = kb.at[pl.ds(pl.multiple_of(src * 512, 512), 512), :]
            b = kb.at[pl.ds(dst * 512, 512), :]
        else:
            a = vb.at[:, pl.ds(pl.multiple_of(src * 512, 512), 512)]
            b = vb.at[:, pl.ds(dst * 512, 512)]
        return remote(a, b, kvs.at[kind, part], kvr.at[kind, part], dev)

    def w_ref(a, b, core):
        return wb.at[(z + a) % 4, (y + b) % 4, core]

    RING, OWN, FWD, PLUS, SHARE = 0, 1, 2, 3, 4

    def w_send(kind, s):
        if kind == RING:
            ref, dev = w_ref(s, 0, c), zm
        elif kind >= SHARE:
            ref, dev = w_ref(s, kind - SHARE, c), sib
        elif kind == OWN or s == 0 or (kind == PLUS and s == 2):
            ref = w_ref(s, 1 if kind == FWD else 0, c)
            dev = yp if kind == PLUS else ym
        else:
            ref = w_ref(1 if s == 2 else 0, kind, c)
            dev = zp if s == 3 else zm
        return remote(ref, ref, ws.at[kind, s], wr.at[kind, s], dev)

    def w_come(kind, s):
        if kind == RING:
            ref = w_ref(s + 1, 0, c)
        elif kind >= SHARE:
            ref = w_ref(s, kind - SHARE, 1 - c)
        else:
            ref = w_ref(s, (0, 1, 2, 3)[kind], c)
        return remote(ref, ref, ws.at[kind, s], wr.at[kind, s], sib)

    def w_own(s):
        w_send(OWN, s).start()
        w_send(SHARE, s).start()

    def w_fwd(s):
        w_come(OWN, s).wait_recv()
        if s == 0:
            w_send(FWD, 0).start()
        w_send(SHARE + 1, s).start()

    def w_ring(s):
        w_come(RING, s - 1).wait_recv()
        if s < 3:
            w_send(RING, s).start()
        w_own(s)

    lv.wait()
    vb[:, 2048:] = jnp.transpose(vv[...].astype(F32)).astype(BF16)

    lane = lax.broadcasted_iota(jnp.int32, (128, 128), 1)
    row = lax.broadcasted_iota(jnp.int32, (128, 128), 0)
    for w in range(20):
        eb[w * 128 : (w + 1) * 128, :] = (lane == w).astype(F32).astype(BF16)
    tri = jnp.where(row <= lane, 0.0, -BIG).astype(F32)
    tri2 = jnp.concatenate([tri, tri], axis=1)
    first_block = d * 4
    block = lax.broadcasted_iota(jnp.int32, (16, 128), 1) + (first_block - 16)
    doc = jnp.zeros((16, 128), jnp.int32)
    own = [jnp.int32(0)] * 4
    end = jnp.int32(0)
    for t in range(NDOC):
        end = end + doc_ref[t]
        doc = doc + (end <= block).astype(jnp.int32)
        own = [own[i] + (end <= first_block + i).astype(jnp.int32) for i in range(4)]
    for i in range(4):
        allowed = (doc == own[i]) & (block >= 0)
        bias[i] = jnp.where(allowed, 0.0, -BIG).astype(BF16)

    lk.wait()
    lw.wait()
    pl.semaphore_wait(barrier, 9)

    kv(0, 0).start()
    kv(0, 1).start()

    @pl.when(c == 0)
    def _():
        kv(2, 0).start()
        kv(2, 1).start()

    w_send(RING, 0).start()
    w_own(0)
    lq.wait()

    def kv_near(part):
        kv(0, part).wait_recv()
        kv(1, part).start()

        @pl.when(c == 0)
        def _():
            kv(3, part).start()

        @pl.when(c == 1)
        def _():
            kv(2, part).start()

    def kv_far(part):
        kv(1, part).wait_recv()

        @pl.when(c == 1)
        def _():
            kv(3, part).start()

    def span(phase, i):
        return ((2048, (i + 1) * 128), (1024, 1024), ((i + 1) * 128, (7 - i) * 128))[phase]

    def scores(phase, hp, i, slot, ck, mx):
        base, total = span(phase, i)
        o, n = chunks(total)[ck]
        q2 = qv[i * 128 : i * 128 + 128, pl.ds(pl.multiple_of(hp * 256, 256), 256)]
        b = jnp.concatenate([bias[i]] * 8, axis=0)
        qq = jnp.concatenate(
            [
                jnp.concatenate([q2[:, :128], b], axis=1),
                jnp.concatenate([q2[:, 128:], b], axis=1),
            ],
            axis=0,
        )
        rows = slice(base + o, base + o + n)
        kk = jnp.concatenate([kb[rows, :], eb[rows, :]], axis=1)
        s = lax.dot_general(kk, qq, NT, preferred_element_type=F32)
        if phase == 0 and o + n == total:
            last = s[n - 128 :] + tri2
            s = last if n == 128 else jnp.concatenate([s[: n - 128], last], axis=0)
        s_buf[slot, o : o + n, :] = s
        new = jnp.max(s.reshape(n // 8, 8, 256), axis=0)
        return new if mx is None else jnp.maximum(mx, new)

    def weigh(phase, i, slot, ck, m, acc):
        base, total = span(phase, i)
        o, n = chunks(total)[ck]
        s = s_buf[slot, o : o + n, :]
        p = jnp.exp2((s - m) * SCALE).astype(BF16)
        lhs = jnp.concatenate([vb[:, base + o : base + o + n], jnp.ones((16, n), BF16)], axis=0)
        t = lax.dot_general(lhs, p, NN, preferred_element_type=F32)
        return t if acc is None else acc + t

    def attention(phase, between):
        def top(hp, i, mx):
            m = jnp.max(mx, axis=0, keepdims=True)
            return m if phase == 0 else jnp.maximum(m, m_buf[hp, i, 0:1, :])

        def one(hp, m):
            for i in range(4):
                slot = i % 2
                nhp, ni = (hp, i + 1) if i < 3 else (jnp.minimum(hp + 1, 3), 0)
                mx, acc = None, None
                na, nb = len(chunks(span(phase, ni)[1])), len(chunks(span(phase, i)[1]))
                for ck in range(max(na, nb)):
                    if ck < na:
                        mx = scores(phase, nhp, ni, 1 - slot, ck, mx)
                    if ck < nb:
                        acc = weigh(phase, i, slot, ck, m, acc)
                acc = acc[:136]
                if phase > 0:
                    alpha = jnp.exp2((m_buf[hp, i, 0:1, :] - m) * SCALE)
                    acc = acc + a_buf[hp, i] * alpha
                if phase < 2:
                    m_buf[hp, i] = jnp.broadcast_to(m, (8, 256))
                    a_buf[hp, i] = acc
                else:
                    out = (acc[:128] / acc[128:129]).astype(BF16)
                    f = pl.multiple_of(hp * 256, 256)
                    att[pl.ds(f, 128), i * 128 : i * 128 + 128] = out[:, :128]
                    att[pl.ds(f + 128, 128), i * 128 : i * 128 + 128] = out[:, 128:]
                m = top(nhp, ni, mx)
            between(hp)
            return m

        mx = None
        for ck in range(len(chunks(span(phase, 0)[1]))):
            mx = scores(phase, 0, 0, 0, ck, mx)
        lax.fori_loop(0, 4, one, top(0, 0, mx))

    attention(0, lambda hp: None)
    w_ring(1)
    kv_near(0)
    kv_near(1)
    w_ring(2)
    w_fwd(0)
    kv(2, 0).wait_recv()
    kv(2, 1).wait_recv()

    def first(hp):
        @pl.when(hp == 0)
        def _():
            w_fwd(1)

        @pl.when(hp == 1)
        def _():
            w_ring(3)

        @pl.when(hp == 2)
        def _():
            kv_far(0)
            w_fwd(2)
            w_come(FWD, 0).wait_recv()
            w_send(FWD, 1).start()
            w_send(SHARE + FWD, 0).start()

    def second(hp):
        @pl.when(hp == 0)
        def _():
            w_fwd(3)

        @pl.when(hp == 1)
        def _():
            w_come(FWD, 1).wait_recv()
            w_send(FWD, 2).start()
            w_send(SHARE + FWD, 1).start()

    attention(1, first)
    kv_far(1)
    w_send(PLUS, 0).start()
    w_send(FWD, 3).start()
    for part in range(2):
        kv(3, part).wait_recv()
    attention(2, second)
    w_come(PLUS, 0).wait_recv()
    w_send(PLUS, 1).start()
    w_send(PLUS, 3).start()
    w_send(PLUS, 2).start()
    w_send(SHARE + PLUS, 0).start()

    lo, hi = pl.ds(0, 64), pl.ds(64, 64)
    left, right, far = (h + 3) % 4, (h + 1) % 4, (h + 2) % 4

    def x_copy(g, k):
        src, dst = (
            (pb.at[g, far, lo], r1p.at[g]),
            (pb.at[g, far, hi], r1m.at[g]),
            (pb.at[g, right, hi], r2p.at[g, hi]),
            (pb.at[g, left, lo], r2m.at[g, lo]),
            (pb.at[g, right, lo], r2p.at[g, lo]),
            (pb.at[g, left, hi], r2m.at[g, hi]),
        )[k]
        return remote(src, dst, xs.at[g, k], xr.at[g, k], (xp, xm)[k % 2])

    def project(b):
        for s in range(4):
            w_come(SHARE + b, s).wait_recv()
        g = (y + b) % 4
        w = wb[:, g].reshape(512, 1024)
        for half in range(2):
            cols = slice(half * 256, half * 256 + 256)
            t = lax.dot_general(w, att[:, cols], NN, preferred_element_type=F32).astype(BF16)
            pb[g, :, :, cols] = t.reshape(4, 128, 256)
        for k in range(4):
            x_copy(g, k).start()

    def merge(b):
        g = (y + b) % 4
        x_copy(g, 0).wait_recv()
        pb[g, right, lo, :] = (pb[g, right, lo, :].astype(F32) + r1p[g].astype(F32)).astype(BF16)
        x_copy(g, 4).start()
        x_copy(g, 1).wait_recv()
        pb[g, left, hi, :] = (pb[g, left, hi, :].astype(F32) + r1m[g].astype(F32)).astype(BF16)
        x_copy(g, 5).start()

    def write(g):
        return pltpu.make_async_copy(
            obuf.at[g], out_hbm.at[:, pl.ds(pl.multiple_of(g * 128, 128), 128)], lsem.at[4 + g]
        )

    def finish(b):
        g = (y + b) % 4
        for k in range(2, 6):
            x_copy(g, k).wait_recv()
        total = pb[g, h].astype(F32) + r2p[g].astype(F32) + r2m[g].astype(F32)
        obuf[g] = jnp.transpose(total).astype(BF16)
        write(g).start()

    def w_last(kind, steps):
        for s in steps:
            w_come(kind, s).wait_recv()
            w_send(SHARE + kind, s).start()

    project(0)
    project(1)
    w_last(FWD, (3, 2))
    w_last(PLUS, (1, 3, 2))
    merge(0)
    merge(1)
    project(2)
    project(3)
    finish(0)
    merge(2)
    finish(1)
    merge(3)
    for kind in range(4):
        for part in range(2):
            kv(kind, part).wait_send()
    for kind in range(SHARE + 4):
        for s in range(3 if kind == RING else 4):
            w_send(kind, s).wait_send()
    finish(2)
    for g in range(3):
        for k in range(4):
            x_copy((y + g) % 4, k).wait_send()
    finish(3)
    for g in range(4):
        write(g).wait()
    for b in range(4):
        for k in range(4 if b < 3 else 0, 6):
            x_copy((y + b) % 4, k).wait_send()


def local(query_rows, key_rows, value_rows, doc_blocks, out_weight):
    hbm = pl.BlockSpec(memory_space=pl.ANY)
    dma = pltpu.SemaphoreType.DMA
    return pl.pallas_call(
        kernel,
        out_shape=jax.ShapeDtypeStruct((512, 512), BF16),
        in_specs=[hbm, hbm, hbm, pl.BlockSpec(memory_space=pltpu.SMEM), hbm],
        out_specs=hbm,
        scratch_shapes=[
            pltpu.VMEM((512, 1024), BF16),
            pltpu.VMEM((2560, 128), BF16),
            pltpu.VMEM((2560, 128), BF16),
            pltpu.VMEM((512, 128), BF16),
            pltpu.VMEM((128, 2560), BF16),
            pltpu.VMEM((4, 16, 128), BF16),
            pltpu.VMEM((4, 4, 2, 64, 1024), BF16),
            pltpu.VMEM((2, 1024, 256), F32),
            pltpu.VMEM((4, 4, 8, 256), F32),
            pltpu.VMEM((4, 4, 136, 256), F32),
            pltpu.VMEM((1024, 512), BF16),
            pltpu.VMEM((4, 4, 128, 512), BF16),
            pltpu.VMEM((4, 64, 512), BF16),
            pltpu.VMEM((4, 64, 512), BF16),
            pltpu.VMEM((4, 128, 512), BF16),
            pltpu.VMEM((4, 128, 512), BF16),
            pltpu.VMEM((4, 512, 128), BF16),
            dma((8,)),
            dma((4, 2)), dma((4, 2)),
            dma((8, 4)), dma((8, 4)),
            dma((4, 6)), dma((4, 6)),
        ],
        compiler_params=pltpu.CompilerParams(
            collective_id=0, has_side_effects=True, vmem_limit_bytes=62 * 2**20
        ),
    )(query_rows, key_rows, value_rows, doc_blocks, out_weight.T)


def solution(mesh):
    placed = (P("docs", "heads"), P("docs", "heads"), P("docs", "heads"), P(), P("heads", "docs"))
    return jax.shard_map(
        local, mesh=mesh, in_specs=placed, out_specs=P("docs", "heads"), check_vma=False
    )
```
